128 devices in a mesh: dp: 8 (over z, core), table: 16 (over x, y).
Axes of the slice: x: 4, y: 4, z: 4, core: 2. Of those that a mesh axis runs over, the one named last changes fastest.
Arguments:
- emb_table: bfloat16 [32768, 128, 128], P(('dp', 'table')), may hold values from -6 to 6
- requests: int32 [16384, 3], P(('dp', 'table')), may hold values from -1 to 255, as said below
- bag_rows: int32 [16777216], P(('dp', 'table')), may hold values from 0 to 49151, as said below
- placement_slot: int32 [524288], P(('dp', 'table')), may hold values from -1 to 2047, as said below
- w_hidden: bfloat16 [2048, 1024], replicated, may hold values from -0.125 to 0.125
- w_out: bfloat16 [1024, 256], replicated, may hold values from -0.1875 to 0.1875
Outputs:
- item_vectors: bfloat16 [262144, 256], P(('dp', 'table'))
The draws below stay inside these ranges and needn't reach their ends.
Inputs may be any that keep to these rules, and one draw needn't show every extreme that they name: `placement_slot`: each device's slots hold -1 for items that are not dirty, else k * 256 + s, sending the item to slot s of index shard k (the device of dp index k in the same table column). No value repeats on one device, the slots s used toward each k run from 0 upward, and in each table column one index shard gets 256 items from every device. In each row (one device, one owner) the live block numbers come first and the -1 entries after them; every device has some owner from which it requests 3 blocks, and owners differ in how many blocks are asked of them. `bag_rows`: every entry names a row of a block slot whose request is not -1.
All inputs are finite; a program needn't handle non-finite values.
Results may differ from the reference program's by a relative error of at most 0.0059.
Values may be sent and summed in bfloat16 or wider, within the bound.
A program may use at most 128 MiB of HBM per device.

```python
import jax
import jax.numpy as jnp
from jax import lax

EMB = 128
BLOCK_ROWS = 128
FEATS = 16
BAG = 2
UNITS = 1024
VEC = 256
CAP = 3
ITEMS_DEV = 4096
BLOCKS_DEV = 256
SEND_CAP = 256
BLOCKS = 32768
N_DP = 8
N_TABLE = 16


def request_counts(key):
    device_count = N_DP * N_TABLE
    count_key = jax.random.fold_in(key, 11)
    base_key, hot_key, sure_key = jax.random.split(count_key, 3)
    base = jax.random.randint(base_key, (device_count, device_count), 0, 3)
    hot = jax.random.randint(hot_key, (device_count, device_count), 0, 4) == 0
    sure = jax.random.randint(sure_key, (device_count,), 0, device_count)
    hot = hot | (jnp.arange(device_count)[None, :] == sure[:, None])
    return jnp.where(hot, CAP, base).astype(jnp.int32)


def draw_requests(key, part):
    counts = request_counts(key)
    key = jax.random.fold_in(key, 3)
    device_count = N_DP * N_TABLE
    numbers = jax.random.randint(key, (device_count, device_count, CAP), 0, BLOCKS_DEV)
    live = jnp.arange(CAP)[None, None, :] < counts[:, :, None]
    return jnp.where(live, numbers, -1).reshape(device_count * device_count, CAP).astype(jnp.int32)


def draw_bag_rows(key, part):
    counts = request_counts(key)
    key = jax.random.fold_in(key, 5)
    device_count = N_DP * N_TABLE
    entries = ITEMS_DEV * FEATS * BAG
    device_keys = jax.random.split(key, device_count)

    def per_device(one_key, owner_counts):
        pick_key, row_key = jax.random.split(one_key)
        ends = jnp.cumsum(owner_counts)
        total = ends[-1]
        chosen = jax.random.randint(pick_key, (entries,), 0, total)
        owner = jnp.searchsorted(ends, chosen, side='right').astype(jnp.int32)
        within = chosen - (ends[owner] - owner_counts[owner])
        row = jax.random.randint(row_key, (entries,), 0, BLOCK_ROWS)
        return (owner * CAP + within) * BLOCK_ROWS + row
    return jax.vmap(per_device)(device_keys, counts).reshape(-1).astype(jnp.int32)


def draw_placement_slot(key, part):
    key = jax.random.fold_in(key, 7)
    device_count = N_DP * N_TABLE
    send_cap = ITEMS_DEV // (2 * N_DP)
    hot_key, device_key = jax.random.split(key)
    hot_shard = jax.random.randint(hot_key, (N_TABLE,), 0, N_DP)
    column = jnp.arange(device_count) % N_TABLE
    hot_target = hot_shard[column]
    device_keys = jax.random.split(device_key, device_count)

    def per_device(one_key, target):
        crowd_key, count_key, order_key = jax.random.split(one_key, 3)
        crowded = jax.random.randint(crowd_key, (), 0, 3) == 0
        counts = jax.random.randint(count_key, (N_DP,), 0, send_cap // 2 + 1)
        counts = jnp.where(crowded, send_cap, counts)
        counts = jnp.where(jnp.arange(N_DP) == target, send_cap, counts)
        shard_grid = jnp.arange(N_DP)[:, None]
        slot_grid = jnp.arange(send_cap)[None, :]
        usable = (slot_grid < counts[:, None]).reshape(-1)
        labels = (shard_grid * send_cap + slot_grid).reshape(-1)
        ranking = jnp.where(usable, 0, 1) * (N_DP * send_cap) + jnp.arange(N_DP * send_cap)
        ordering = jnp.argsort(ranking, stable=True)
        packed = jnp.where(usable[ordering], labels[ordering], -1)
        filled = jnp.concatenate([packed, jnp.full((ITEMS_DEV - N_DP * send_cap,), -1, packed.dtype)])
        return filled[jax.random.permutation(order_key, ITEMS_DEV)]
    return jax.vmap(per_device)(device_keys, hot_target).reshape(-1).astype(jnp.int32)


def steps_of(own_key, shape, shards, least, largest):
    level = 1.0
    for axis_at, blocks in shards:
        draws = jax.random.uniform(jax.random.fold_in(jax.random.fold_in(own_key, 6), axis_at), (blocks,), jnp.float32, least / len(shards), largest / len(shards))
        level = level * jnp.repeat(jnp.exp(draws), shape[axis_at] // blocks).reshape((-1,) + (1,) * (len(shape) - 1 - axis_at))
    return level


def noise(key, extent, scale, bound, pieces=(), kind=jnp.bfloat16):
    factor_of = steps_of(key, extent, pieces, -0.22, 0.18) if pieces else 1.0
    values = jax.random.normal(key, extent, jnp.float32) * scale * factor_of
    return jnp.minimum(jnp.maximum(values, -bound), bound).astype(kind)


def setup_inputs(seed: int = 0) -> dict:
    key_of = jax.random.split(jax.random.key(seed), 7)
    return {
        "emb_table": noise(key_of[0], (BLOCKS, BLOCK_ROWS, EMB), 1.0, 6.0, ((0, 128),)),
        "requests": draw_requests(jax.random.fold_in(key_of[6], 71), 0),
        "bag_rows": draw_bag_rows(jax.random.fold_in(key_of[6], 71), 0),
        "placement_slot": draw_placement_slot(jax.random.fold_in(key_of[6], 71), 0),
        "w_hidden": noise(key_of[4], (FEATS * EMB, UNITS), (FEATS * EMB) ** -0.5, 0.125),
        "w_out": noise(key_of[5], (UNITS, VEC), UNITS ** -0.5, 0.1875),
    }


def item_tower(inputs, w_hidden, w_out):
    hidden = jnp.maximum(jnp.dot(inputs, w_hidden, preferred_element_type=jnp.float32), 0.0).astype(jnp.bfloat16)
    raw = jnp.dot(hidden, w_out, preferred_element_type=jnp.float32)
    scale = lax.rsqrt(lax.optimization_barrier(jnp.mean(raw * raw, axis=-1, keepdims=True)) + 1e-06)
    return (raw * scale).astype(jnp.bfloat16)

def reference(emb_table, requests, bag_rows, placement_slot, w_hidden, w_out):
    device_count = N_DP * N_TABLE
    width = FEATS * EMB
    owner_base = (jnp.arange(device_count, dtype=jnp.int32) * BLOCKS_DEV)[:, None]
    wanted = requests.reshape(device_count, device_count, CAP)
    bag_table = bag_rows.reshape(device_count, ITEMS_DEV * FEATS * BAG)
    slot_table = placement_slot.reshape(device_count, ITEMS_DEV)

    def per_device(packed):
        block_ids, bag_ids, slot_ids = packed
        live = block_ids >= 0
        global_ids = jnp.where(live, block_ids + owner_base, 0).reshape(-1).astype(jnp.int32)
        blocks = jnp.take(emb_table, global_ids, axis=0)
        blocks = jnp.where(live.reshape(-1)[:, None, None], blocks, jnp.zeros_like(blocks))
        fetched = blocks.reshape(-1, EMB)
        picked = jnp.take(fetched, bag_ids, axis=0).reshape(ITEMS_DEV, FEATS, BAG, EMB)
        pooled = lax.optimization_barrier(jnp.sum(picked.astype(jnp.float32), axis=2)).reshape(ITEMS_DEV, width).astype(jnp.bfloat16)
        target = jnp.where(slot_ids >= 0, slot_ids, N_DP * SEND_CAP).astype(jnp.int32)
        outgoing = jnp.zeros((N_DP * SEND_CAP, width), jnp.bfloat16).at[target].set(pooled, mode='drop')
        return outgoing.reshape(N_DP, SEND_CAP, width)
    outgoing_all = lax.map(per_device, (wanted, bag_table, slot_table))
    arranged = outgoing_all.reshape(N_DP, N_TABLE, N_DP, SEND_CAP, width)
    arranged = jnp.transpose(arranged, (2, 1, 0, 3, 4)).reshape(device_count, N_DP * SEND_CAP, width)

    def run_tower(block_inputs):
        return item_tower(block_inputs, w_hidden, w_out)
    vectors = lax.map(run_tower, arranged)
    return vectors.reshape(device_count * N_DP * SEND_CAP, VEC)
```

```python
import itertools

import jax
import jax.numpy as jnp
import numpy as np
from jax import lax
from jax.experimental import pallas as pl
from jax.experimental.pallas import tpu as pltpu
from jax.sharding import PartitionSpec as P

MESH = pl.DeviceIdType.MESH
FEATS = 16
N_DP, N_TABLE = 8, 16
DEVICES = N_DP * N_TABLE
CAP = 3
ROWS = 128
EMB = 128
ITEMS = 4096
SLOTS = 2048
GROUP = 256
GROUPS = SLOTS * FEATS // GROUP
SHARD = SLOTS // N_DP
UNITS = 1024
VEC = 256
TABLE_ROWS = CAP * DEVICES * ROWS
ZERO_ROW = TABLE_ROWS

DISPLACEMENTS = [d for d in itertools.product(range(4), range(4), range(4), range(2)) if any(d)]


def hops(d):
    load = np.zeros(6)
    for axis in range(3):
        if d[axis] in (1, 2):
            load[2 * axis] += 1
        if d[axis] in (2, 3):
            load[2 * axis + 1] += 1
    return load


def balanced(left):
    left, out, total = list(left), [], np.zeros(6)
    mean = sum(hops(d).sum() for d in left) / len(left)
    rng = np.random.default_rng(0)

    def score(d):
        after = total + hops(d)
        value = 10 * (after.max() - after.min()) + ((after - after.mean()) ** 2).sum()
        return value + 0.3 * abs(after.sum() / (len(out) + 1) - mean) + 0.01 * rng.random()

    while left:
        best = min([(score(d), d) for d in left])[1]
        left.remove(best)
        out.append(best)
        total = total + hops(best)
    return out


def part_of(d):
    return ((d[1] - d[0]) % 4) * 2 + d[3]


def place_of(d):
    return part_of(d) * 16 + d[0] * 4 + (d[2] - d[0]) % 4


ORDER = balanced(DISPLACEMENTS)
ORDER_BY_PART = sum([balanced([d for d in DISPLACEMENTS if part_of(d) == k]) for k in range(8)], [])


def my_place():
    i, j = lax.axis_index("dp"), lax.axis_index("table")
    return lax.div(j, 4), lax.rem(j, 4), lax.div(i, 2), lax.rem(i, 2)


def moved(d, sign):
    x, y, z, core = my_place()
    x = lax.rem(x + (sign * d[0]) % 4, 4)
    y = lax.rem(y + (sign * d[1]) % 4, 4)
    z = lax.rem(z + (sign * d[2]) % 4, 4)
    core = lax.rem(core + d[3], 2)
    return z * 2 + core, x * 4 + y


def table_row(idx, present):
    x, y, z, core = my_place()
    block = idx >> 7
    owner = (block * 43691) >> 17
    slot = block - owner * 3
    dx = (x - ((owner >> 2) & 3)) & 3
    dy = (y - (owner & 3)) & 3
    dz = (z - (owner >> 5)) & 3
    dcore = (core - ((owner >> 4) & 1)) & 1
    part = ((dy - dx) & 3) * 2 + dcore
    place = part * 16 + dx * 4 + ((dz - dx) & 3)
    row = ((slot * DEVICES + place) << 7) | (idx & 127)
    return jnp.where(present, row, ZERO_ROW), jnp.where(present, jnp.where(slot == 2, slot + part, slot), 0)


def pick_bags(bags_ref, placed_ref, bag_t, picked):
    bag_t[...] = jnp.transpose(bags_ref[...])
    ones = jnp.ones((8, 1024), jnp.float32)

    def chunk(n, _):
        lane = lax.broadcasted_iota(jnp.int32, (1024, 256), 1) + n * 256
        wanted = (lane & 127) * 16 + (lane >> 7)
        total = jnp.zeros((72, 256), jnp.float32)
        for q in range(4):
            hit = placed_ref[:, q : q + 1] == wanted
            hit = jnp.where(hit, 1.0, 0.0).astype(jnp.bfloat16)
            bag = bag_t[q * 32 : (q + 1) * 32, :]
            left = jnp.concatenate([(bag >> 8).astype(jnp.float32), (bag & 255).astype(jnp.float32), ones])
            total += jnp.dot(left.astype(jnp.bfloat16), hit, preferred_element_type=jnp.float32)
        picked[2 * n] = total[:, :128]
        picked[2 * n + 1] = total[:, 128:]
        return 0

    lax.fori_loop(0, SLOTS // 256, chunk, 0)


def bag_matrix(picked, entry):
    rows, live = [], []
    for t in range(16):
        high = picked[t, pl.ds(entry, 16, stride=2), :]
        low = picked[t, pl.ds(32 + entry, 16, stride=2), :]
        rows.append(high.astype(jnp.int32) * 256 + low.astype(jnp.int32))
        there = picked[t, 64:72, :] > 0.5
        live.append(jnp.concatenate([jnp.where(there, 1, 0)] * 2))
    return jnp.concatenate(rows), jnp.concatenate(live) > 0


def fetch_kernel(
    emb, req, bags, placed, fetched, row_a, row_b,
    emb_v, staged, req_in, req_s, bag_t, picked,
    emb_sem, req_send, req_recv, own_sem, send_sem, recv_sem,
):
    me_dp, me_table = lax.axis_index("dp"), lax.axis_index("table")
    load = pltpu.make_async_copy(emb, emb_v, emb_sem)
    load.start()
    barrier = pltpu.get_barrier_semaphore()
    for d in ORDER:
        pl.semaphore_signal(barrier, inc=1, device_id=moved(d, 1), device_id_type=MESH)
    pl.semaphore_wait(barrier, DEVICES - 1)

    own = pltpu.make_async_copy(req.at[me_dp * N_TABLE + me_table], req_in.at[0], own_sem)
    own.start()
    for d in ORDER:
        to = moved(d, -1)
        pltpu.make_async_remote_copy(
            src_ref=req.at[to[0] * N_TABLE + to[1]], dst_ref=req_in.at[place_of(d)],
            send_sem=req_send, recv_sem=req_recv, device_id=to, device_id_type=MESH,
        ).start()
    own.wait()
    others = req_in.at[pl.ds(1, DEVICES - 1)]
    pltpu.make_async_copy(others, others, req_recv).wait()
    pltpu.make_async_copy(others, others, req_send).wait()
    numbers = pltpu.make_async_copy(req_in, req_s, own_sem)
    numbers.start()
    load.wait()
    numbers.wait()

    for slot in range(CAP):

        def serve(n, _):
            number = req_s[n, 0, slot]
            block = emb_v[jnp.maximum(number, 0)]
            staged[slot, n] = jnp.where(number >= 0, block, jnp.zeros_like(block))
            return 0

        lax.fori_loop(0, DEVICES, serve, 0)
        for d in ORDER if slot < 2 else ORDER_BY_PART:
            n = place_of(d)
            pltpu.make_async_remote_copy(
                src_ref=staged.at[slot, n], dst_ref=fetched.at[slot, n],
                send_sem=send_sem, recv_sem=recv_sem, device_id=moved(d, 1), device_id_type=MESH,
            ).start()
    mine = pltpu.make_async_copy(staged.at[:, 0], fetched.at[:, 0], own_sem)
    mine.start()

    pick_bags(bags, placed, bag_t, picked)
    for entry, out in ((0, row_a), (1, row_b)):
        idx, present = bag_matrix(picked, entry)
        out[...] = table_row(idx, present)[0]

    mine.wait()
    arrived = fetched.at[:, pl.ds(1, DEVICES - 1)]
    pltpu.make_async_copy(arrived, arrived, recv_sem).wait()
    sent = staged.at[:, pl.ds(1, DEVICES - 1)]
    pltpu.make_async_copy(sent, sent, send_sem).wait()


def fetch(emb_table, requests, bag_rows, placement_slot):
    req = jnp.pad(requests, ((0, 0), (0, 125))).reshape(DEVICES, 1, 128)
    hbm = pl.BlockSpec(memory_space=pl.ANY)
    vmem = pl.BlockSpec(memory_space=pltpu.VMEM)
    return pl.pallas_call(
        fetch_kernel,
        in_specs=[hbm, vmem, vmem, vmem],
        out_specs=(hbm, vmem, vmem),
        out_shape=(
            jax.ShapeDtypeStruct((CAP, DEVICES, ROWS, EMB), jnp.bfloat16),
            jax.ShapeDtypeStruct((GROUP, GROUPS), jnp.int32),
            jax.ShapeDtypeStruct((GROUP, GROUPS), jnp.int32),
        ),
        scratch_shapes=[
            pltpu.VMEM((256, ROWS, EMB), jnp.bfloat16),
            pltpu.VMEM((CAP, DEVICES, ROWS, EMB), jnp.bfloat16),
            pltpu.VMEM((DEVICES, 1, 128), jnp.int32),
            pltpu.SMEM((DEVICES, 1, 128), jnp.int32),
            pltpu.VMEM((128, 1024), jnp.int32),
            pltpu.VMEM((16, 72, 128), jnp.float32),
        ]
        + [pltpu.SemaphoreType.DMA] * 6,
        compiler_params=pltpu.CompilerParams(
            collective_id=1, has_side_effects=True, vmem_limit_bytes=58 * 2**20
        ),
        name="fetch_blocks",
    )(emb_table, req, bag_rows.reshape(1024, 128), placement_slot.reshape(1024, 4))


def tower(x, w_hidden, w_out):
    hidden = jnp.maximum(jnp.dot(x, w_hidden, preferred_element_type=jnp.float32), 0.0).astype(jnp.bfloat16)
    raw = jnp.dot(hidden, w_out, preferred_element_type=jnp.float32)
    scale = lax.rsqrt(jnp.mean(raw * raw, axis=-1, keepdims=True) + 1e-06)
    return (raw * scale).astype(jnp.bfloat16)


def pool_kernel(row_a, row_b, fetched, w_hidden, w_out, out, table, rows, x, chunk, sem):
    step = pl.program_id(0)

    @pl.when(step == 0)
    def _():
        table[pl.ds(ZERO_ROW, 8), :] = jnp.zeros((8, EMB), jnp.float32)
        pieces = CAP * DEVICES // 16

        def copy(n):
            return pltpu.make_async_copy(
                fetched.at[lax.div(n, 8), pl.ds(lax.rem(n, 8) * 16, 16)], chunk.at[lax.rem(n, 2)], sem.at[lax.rem(n, 2)]
            )

        copy(0).start()

        def load(n, _):
            @pl.when(n + 1 < pieces)
            def _():
                copy(n + 1).start()

            copy(n).wait()
            for k in range(16):
                at = pl.multiple_of((n * 16 + k) * ROWS, ROWS)
                table[pl.ds(at, ROWS), :] = chunk[lax.rem(n, 2), k].astype(jnp.float32)
            return 0

        lax.fori_loop(0, pieces, load, 0)

    def group(g, _):
        def some(t, _):
            for f in range(FEATS):
                a = row_a[t * FEATS + f, step * 16 + g]
                b = row_b[t * FEATS + f, step * 16 + g]
                rows[pl.ds(f * 16 + t, 1), :] = table[pl.ds(a, 1), :] + table[pl.ds(b, 1), :]
            return 0

        lax.fori_loop(0, 16, some, 0, unroll=2)
        at = pl.multiple_of(g * 16, 16)
        for f in range(FEATS):
            x[pl.ds(at, 16), f * EMB : (f + 1) * EMB] = rows[f * 16 : (f + 1) * 16, :].astype(jnp.bfloat16)
        return 0

    lax.fori_loop(0, 16, group, 0)
    out[...] = tower(x[...], w_hidden[...], w_out[...])


def pool(row_a, row_b, fetched, w_hidden, w_out):
    smem = pl.BlockSpec(memory_space=pltpu.SMEM)
    return pl.pallas_call(
        pool_kernel,
        grid=(N_DP,),
        in_specs=[
            smem,
            smem,
            pl.BlockSpec(memory_space=pl.ANY),
            pl.BlockSpec((2048, UNITS), lambda n: (0, 0), pipeline_mode=pl.Buffered(1)),
            pl.BlockSpec((UNITS, VEC), lambda n: (0, 0), pipeline_mode=pl.Buffered(1)),
        ],
        out_specs=pl.BlockSpec((SHARD, VEC), lambda n: (n, 0)),
        out_shape=jax.ShapeDtypeStruct((SLOTS, VEC), jnp.bfloat16),
        scratch_shapes=[
            pltpu.VMEM((TABLE_ROWS + 8, EMB), jnp.float32),
            pltpu.VMEM((GROUP, EMB), jnp.float32),
            pltpu.VMEM((SHARD, FEATS * EMB), jnp.bfloat16),
            pltpu.VMEM((2, 16, ROWS, EMB), jnp.bfloat16),
            pltpu.SemaphoreType.DMA((2,)),
        ],
        compiler_params=pltpu.CompilerParams(vmem_limit_bytes=58 * 2**20),
        name="pool_and_tower",
    )(row_a, row_b, fetched, w_hidden, w_out)


def local(emb_table, requests, bag_rows, placement_slot, w_hidden, w_out):
    fetched, row_a, row_b = fetch(emb_table, requests, bag_rows, placement_slot)
    vectors = pool(row_a, row_b, fetched, w_hidden, w_out).reshape(N_DP, SHARD, VEC)
    vectors = lax.all_to_all(vectors, "dp", split_axis=0, concat_axis=0, tiled=True)
    return vectors.reshape(SLOTS, VEC)


def solution(mesh):
    placed = (
        P(("dp", "table"), None, None),
        P(("dp", "table"), None),
        P(("dp", "table")),
        P(("dp", "table")),
        P(),
        P(),
    )
    return jax.shard_map(
        local, mesh=mesh, in_specs=placed, out_specs=P(("dp", "table"), None), check_vma=False
    )
```

```python
import itertools

import jax
import jax.numpy as jnp
import numpy as np
from jax import lax
from jax.experimental import pallas as pl
from jax.experimental.pallas import tpu as pltpu
from jax.sharding import PartitionSpec as P

MESH = pl.DeviceIdType.MESH
FEATS = 16
N_DP, N_TABLE = 8, 16
DEVICES = N_DP * N_TABLE
CAP = 3
ROWS = 128
EMB = 128
ITEMS = 4096
SLOTS = 2048
GROUP = 256
GROUPS = SLOTS * FEATS // GROUP
SHARD = SLOTS // N_DP
UNITS = 1024
VEC = 256
TABLE_ROWS = CAP * DEVICES * ROWS
ZERO_ROW = TABLE_ROWS

PHASES = 13
SCHEDULE = (16, 32, 48, 80, 112, 112, 128, 144, 144, 160, 176, 192, GROUP)

DISPLACEMENTS = [d for d in itertools.product(range(4), range(4), range(4), range(2)) if any(d)]


def hops(d):
    load = np.zeros(6)
    for axis in range(3):
        if d[axis] in (1, 2):
            load[2 * axis] += 1
        if d[axis] in (2, 3):
            load[2 * axis + 1] += 1
    return load


def balanced(left):
    left, out, total = list(left), [], np.zeros(6)
    mean = sum(hops(d).sum() for d in left) / len(left)
    rng = np.random.default_rng(0)

    def score(d):
        after = total + hops(d)
        value = 10 * (after.max() - after.min()) + ((after - after.mean()) ** 2).sum()
        return value + 0.3 * abs(after.sum() / (len(out) + 1) - mean) + 0.01 * rng.random()

    while left:
        best = min([(score(d), d) for d in left])[1]
        left.remove(best)
        out.append(best)
        total = total + hops(best)
    return out


def part_of(d):
    return ((d[1] - d[0]) % 4) * 2 + d[3]


def place_of(d):
    return part_of(d) * 16 + d[0] * 4 + (d[2] - d[0]) % 4


ORDER = balanced(DISPLACEMENTS)
ORDER_BY_PART = sum([balanced([d for d in DISPLACEMENTS if part_of(d) == k]) for k in range(8)], [])


def my_place():
    i, j = lax.axis_index("dp"), lax.axis_index("table")
    return lax.div(j, 4), lax.rem(j, 4), lax.div(i, 2), lax.rem(i, 2)


def moved(d, sign):
    x, y, z, core = my_place()
    x = lax.rem(x + (sign * d[0]) % 4, 4)
    y = lax.rem(y + (sign * d[1]) % 4, 4)
    z = lax.rem(z + (sign * d[2]) % 4, 4)
    core = lax.rem(core + d[3], 2)
    return z * 2 + core, x * 4 + y


def table_row(idx, present):
    x, y, z, core = my_place()
    block = idx >> 7
    owner = (block * 43691) >> 17
    slot = block - owner * 3
    dx = (x - ((owner >> 2) & 3)) & 3
    dy = (y - (owner & 3)) & 3
    dz = (z - (owner >> 5)) & 3
    dcore = (core - ((owner >> 4) & 1)) & 1
    part = ((dy - dx) & 3) * 2 + dcore
    place = part * 16 + dx * 4 + ((dz - dx) & 3)
    row = ((slot * DEVICES + place) << 7) | (idx & 127)
    phase = jnp.where(slot == 2, 5 + part, jnp.where(slot == 1, 1 + (part >> 1), 0))
    return jnp.where(present, row, ZERO_ROW), jnp.where(present, phase, 0)


def pick_bags(bags_ref, placed_ref, bag_t, picked):
    bag_t[...] = jnp.transpose(bags_ref[...])
    ones = jnp.ones((8, 1024), jnp.float32)

    def chunk(n, _):
        lane = lax.broadcasted_iota(jnp.int32, (1024, 256), 1) + n * 256
        wanted = (lane & 127) * 16 + (lane >> 7)
        total = jnp.zeros((72, 256), jnp.float32)
        for q in range(4):
            hit = placed_ref[:, q : q + 1] == wanted
            hit = jnp.where(hit, 1.0, 0.0).astype(jnp.bfloat16)
            bag = bag_t[q * 32 : (q + 1) * 32, :]
            left = jnp.concatenate([(bag >> 8).astype(jnp.float32), (bag & 255).astype(jnp.float32), ones])
            total += jnp.dot(left.astype(jnp.bfloat16), hit, preferred_element_type=jnp.float32)
        picked[2 * n] = total[:, :128]
        picked[2 * n + 1] = total[:, 128:]
        return 0

    lax.fori_loop(0, SLOTS // 256, chunk, 0)


def bag_matrix(picked, entry):
    rows, live = [], []
    for t in range(16):
        high = picked[t, pl.ds(entry, 16, stride=2), :]
        low = picked[t, pl.ds(32 + entry, 16, stride=2), :]
        rows.append(high.astype(jnp.int32) * 256 + low.astype(jnp.int32))
        there = picked[t, 64:72, :] > 0.5
        live.append(jnp.concatenate([jnp.where(there, 1, 0)] * 2))
    return jnp.concatenate(rows), jnp.concatenate(live) > 0


def sort_rows(key, load):
    row = lax.broadcasted_iota(jnp.int32, (GROUP, GROUPS), 0)
    size = 2
    while size <= GROUP:
        step = size // 2
        while step:
            lower = (row & step) == 0
            other_key = jnp.where(lower, pltpu.roll(key, GROUP - step, 0), pltpu.roll(key, step, 0))
            other_load = jnp.where(lower, pltpu.roll(load, GROUP - step, 0), pltpu.roll(load, step, 0))
            keeps_least = lower == ((row & size) == 0)
            swap = keeps_least == (other_key < key)
            key = jnp.where(swap, other_key, key)
            load = jnp.where(swap, other_load, load)
            step //= 2
        size *= 2
    return key, load


def fused_kernel(
    emb, req, bags, placed, w_hidden, w_out,
    out, fetched, row_a, row_b, late,
    blocks, staged, table, req_in, req_s, bag_t, picked, sorted_a, sorted_b, order_t, rows_a, rows_b,
    chunk, rows, x, vectors, flags,
    emb_sem, req_send, req_recv, own_sem, send_sem, recv_sem, chunk_sem, flag_send, flag_recv, vec_send, vec_recv,
):
    me_dp, me_table = lax.axis_index("dp"), lax.axis_index("table")
    load = pltpu.make_async_copy(emb, blocks, emb_sem)
    load.start()
    barrier = pltpu.get_barrier_semaphore()
    for d in ORDER:
        pl.semaphore_signal(barrier, inc=1, device_id=moved(d, 1), device_id_type=MESH)
    pl.semaphore_wait(barrier, DEVICES - 1)

    own = pltpu.make_async_copy(req.at[me_dp * N_TABLE + me_table], req_in.at[0], own_sem)
    own.start()
    for d in ORDER:
        to = moved(d, -1)
        pltpu.make_async_remote_copy(
            src_ref=req.at[to[0] * N_TABLE + to[1]], dst_ref=req_in.at[place_of(d)],
            send_sem=req_send, recv_sem=req_recv, device_id=to, device_id_type=MESH,
        ).start()
    own.wait()
    others = req_in.at[pl.ds(1, DEVICES - 1)]
    pltpu.make_async_copy(others, others, req_recv).wait()
    pltpu.make_async_copy(others, others, req_send).wait()
    numbers = pltpu.make_async_copy(req_in, req_s, own_sem)
    numbers.start()
    load.wait()
    numbers.wait()

    def send(slot):
        room = slot % 2

        def serve(n, _):
            number = req_s[n, 0, slot]
            block = blocks[jnp.maximum(number, 0)]
            staged[room, n] = jnp.where(number >= 0, block, jnp.zeros_like(block))
            return 0

        lax.fori_loop(0, DEVICES, serve, 0)
        for d in ORDER_BY_PART if slot else ORDER:
            n = place_of(d)
            phase = (0, 1 + part_of(d) // 2, 5 + part_of(d))[slot]
            pltpu.make_async_remote_copy(
                src_ref=staged.at[room, n], dst_ref=fetched.at[slot, n], send_sem=send_sem.at[slot],
                recv_sem=recv_sem.at[phase], device_id=moved(d, 1), device_id_type=MESH,
            ).start()
        mine = pltpu.make_async_copy(staged.at[room, 0], fetched.at[slot, 0], own_sem)
        mine.start()
        mine.wait()

    def sent(slot):
        room = staged.at[slot % 2, pl.ds(1, DEVICES - 1)]
        pltpu.make_async_copy(room, room, send_sem.at[slot]).wait()

    send(0)
    send(1)

    table[pl.ds(ZERO_ROW, 8), :] = jnp.zeros((8, EMB), jnp.float32)
    pick_bags(bags, placed, bag_t, picked)
    idx_a, present = bag_matrix(picked, 0)
    idx_b, _ = bag_matrix(picked, 1)
    idx_a, phase_a = table_row(idx_a, present)
    idx_b, phase_b = table_row(idx_b, present)
    row_a[...] = idx_a
    row_b[...] = idx_b
    row = lax.broadcasted_iota(jnp.int32, (GROUP, GROUPS), 0)
    key = jnp.maximum(phase_a, phase_b) * GROUP + (row & 15) * 16 + (row >> 4)
    key, pair = sort_rows(key, idx_a | (idx_b << 16))
    sorted_a[...] = jnp.minimum(pair & 65535, ZERO_ROW)
    sorted_b[...] = jnp.minimum((pair >> 16) & 65535, ZERO_ROW)
    order_t[...] = jnp.transpose(key & (GROUP - 1))
    to_a = pltpu.make_async_copy(sorted_a, rows_a, chunk_sem.at[0])
    to_b = pltpu.make_async_copy(sorted_b, rows_b, chunk_sem.at[1])
    to_a.start()
    to_b.start()
    limit = jnp.zeros_like(row)
    for end in SCHEDULE[:-1]:
        limit += jnp.where(row >= end, 1, 0)
    missed = jnp.where((key >> 8) > limit, 1, 0)
    flags[0] = jnp.broadcast_to(jnp.max(missed, axis=0, keepdims=True), (8, GROUPS))
    to_a.wait()
    to_b.wait()

    def share(first, count, device):
        copies = []
        for s in range(1, count):
            copies.append(
                pltpu.make_async_remote_copy(
                    src_ref=flags.at[first], dst_ref=flags.at[first + s], send_sem=flag_send.at[first + s],
                    recv_sem=flag_recv.at[first + s], device_id=device(s), device_id_type=MESH,
                )
            )
            copies[-1].start()
        return copies

    def gather_flags(copies, first, count):
        for c in copies:
            c.wait()
        total = flags[first]
        for s in range(1, count):
            total = jnp.maximum(total, flags[first + s])
        return total

    def arrive(slot, first, count):
        pieces = count // 16

        def copy(n):
            return pltpu.make_async_copy(
                fetched.at[slot, pl.ds(first + n * 16, 16)], chunk.at[lax.rem(n, 2)], chunk_sem.at[lax.rem(n, 2)]
            )

        def convert(n):
            copy(n).wait()
            for k in range(16):
                at = pl.multiple_of((slot * DEVICES + first + n * 16 + k) * ROWS, ROWS)
                table[pl.ds(at, ROWS), :] = chunk[lax.rem(n, 2), k].astype(jnp.float32)

        copy(0).start()

        def piece(n, _):
            copy(n + 1).start()
            convert(n)
            return 0

        lax.fori_loop(0, pieces - 1, piece, 0)
        convert(pieces - 1)

    def add_rows(g, low, high, at):
        for n in range(low, high):
            a, b = rows_a[n, g], rows_b[n, g]
            rows[at, n - low : n - low + 1, :] = table[pl.ds(a, 1), :] + table[pl.ds(b, 1), :]

    def pool_some(low, high):
        half, first = low // 128, low % 128
        step = 2 if high - low < 32 else 1

        def eight(n, _):
            def one(m, _):
                for k in range(step):
                    add_rows(n * 8 + m * step + k, low, high, m * step + k)
                return 0

            lax.fori_loop(0, 8 // step, one, 0)
            for m in range(8):
                blocks[(n * 8 + m) * 2 + half, first : first + high - low, :] = rows[m, : high - low, :].astype(
                    jnp.bfloat16
                )
            return 0

        lax.fori_loop(0, GROUPS // 8, eight, 0)

    def phase_done(phase):
        if phase == 0:
            slot, first, count = 0, 0, DEVICES
        elif phase < 5:
            slot, first, count = 1, (phase - 1) * 32, 32
        else:
            slot, first, count = 2, (phase - 5) * 16, 16
        skip = 1 if first == 0 else 0
        arrived = fetched.at[slot, pl.ds(first + skip, count - skip)]
        pltpu.make_async_copy(arrived, arrived, recv_sem.at[phase]).wait()
        arrive(slot, first, count)

    flag_copies = share(0, N_DP, lambda s: (lax.rem(me_dp + s, N_DP), me_table))
    done = 0
    for phase in range(PHASES - 1):
        phase_done(phase)
        if phase == 0:
            sent(0)
            send(2)
        if SCHEDULE[phase] > done:
            pool_some(done, SCHEDULE[phase])
            done = SCHEDULE[phase]
    phase_done(PHASES - 1)
    flags[8] = gather_flags(flag_copies, 0, N_DP)
    flag_copies = share(8, N_TABLE, lambda s: (me_dp, lax.rem(me_table + s, N_TABLE)))

    lane = lax.broadcasted_iota(jnp.int32, (GROUP, GROUP), 0)

    def shard(s, _):
        k = lax.rem(me_dp + 1 + s, N_DP)

        def last_rows(n, _):
            def one(m, _):
                add_rows(k * 16 + n * 8 + m, done, GROUP, m)
                return 0

            lax.fori_loop(0, 8, one, 0)
            for m in range(8):
                blocks[(k * 16 + n * 8 + m) * 2 + 1, done - 128 :, :] = rows[m, : GROUP - done, :].astype(jnp.bfloat16)
            return 0

        lax.fori_loop(0, 2, last_rows, 0)

        def in_place(n, _):
            for m in range(4):
                g = k * 16 + n * 4 + m
                pick = jnp.where(order_t[pl.ds(g, 1), :] == lane, 1.0, 0.0).astype(jnp.bfloat16)
                pooled = jnp.concatenate([blocks[2 * g], blocks[2 * g + 1]])
                pooled = jnp.dot(pick, pooled, preferred_element_type=jnp.float32).astype(jnp.bfloat16)
                at = pl.multiple_of((n * 4 + m) * 16, 16)
                for f in range(FEATS):
                    x[pl.ds(at, 16), f * EMB : (f + 1) * EMB] = pooled[f * 16 : (f + 1) * 16, :]
            return 0

        lax.fori_loop(0, 4, in_place, 0)
        vectors[k] = tower(x[...], w_hidden[...], w_out[...])

        @pl.when(s < N_DP - 1)
        def _():
            pltpu.make_async_remote_copy(
                src_ref=vectors.at[k], dst_ref=out.at[me_dp], send_sem=vec_send.at[s],
                recv_sem=vec_recv.at[me_dp], device_id=(k, me_table), device_id_type=MESH,
            ).start()

        return 0

    lax.fori_loop(0, N_DP, shard, 0)
    late[...] = gather_flags(flag_copies, 8, N_TABLE)
    last = pltpu.make_async_copy(vectors.at[me_dp], out.at[me_dp], own_sem)
    last.start()
    sent(1)
    sent(2)
    for s in range(1, N_DP):
        k = lax.rem(me_dp + s, N_DP)
        pltpu.make_async_copy(vectors.at[k], vectors.at[k], vec_send.at[s - 1]).wait()
        pltpu.make_async_copy(out.at[k], out.at[k], vec_recv.at[k]).wait()
    last.wait()


def fused(emb_table, requests, bag_rows, placement_slot, w_hidden, w_out):
    req = jnp.pad(requests, ((0, 0), (0, 125))).reshape(DEVICES, 1, 128)
    hbm = pl.BlockSpec(memory_space=pl.ANY)
    vmem = pl.BlockSpec(memory_space=pltpu.VMEM)
    dma = pltpu.SemaphoreType.DMA
    return pl.pallas_call(
        fused_kernel,
        in_specs=[hbm, vmem, vmem, vmem, vmem, vmem],
        out_specs=(hbm, hbm, vmem, vmem, vmem),
        out_shape=(
            jax.ShapeDtypeStruct((N_DP, SHARD, VEC), jnp.bfloat16),
            jax.ShapeDtypeStruct((CAP, DEVICES, ROWS, EMB), jnp.bfloat16),
            jax.ShapeDtypeStruct((GROUP, GROUPS), jnp.int32),
            jax.ShapeDtypeStruct((GROUP, GROUPS), jnp.int32),
            jax.ShapeDtypeStruct((8, GROUPS), jnp.int32),
        ),
        scratch_shapes=[
            pltpu.VMEM((256, ROWS, EMB), jnp.bfloat16),
            pltpu.VMEM((2, DEVICES, ROWS, EMB), jnp.bfloat16),
            pltpu.VMEM((TABLE_ROWS + 8, EMB), jnp.float32),
            pltpu.VMEM((DEVICES, 1, 128), jnp.int32),
            pltpu.SMEM((DEVICES, 1, 128), jnp.int32),
            pltpu.VMEM((128, 1024), jnp.int32),
            pltpu.VMEM((16, 72, 128), jnp.float32),
            pltpu.VMEM((GROUP, GROUPS), jnp.int32),
            pltpu.VMEM((GROUP, GROUPS), jnp.int32),
            pltpu.VMEM((GROUPS, GROUP), jnp.int32),
            pltpu.SMEM((GROUP, GROUPS), jnp.int32),
            pltpu.SMEM((GROUP, GROUPS), jnp.int32),
            pltpu.VMEM((2, 16, ROWS, EMB), jnp.bfloat16),
            pltpu.VMEM((8, 96, EMB), jnp.float32),
            pltpu.VMEM((SHARD, FEATS * EMB), jnp.bfloat16),
            pltpu.VMEM((N_DP, SHARD, VEC), jnp.bfloat16),
            pltpu.VMEM((24, 8, GROUPS), jnp.int32),
            dma, dma, dma, dma, dma((CAP,)),
            dma((PHASES,)), dma((2,)), dma((24,)), dma((24,)), dma((N_DP,)), dma((N_DP,)),
        ],
        compiler_params=pltpu.CompilerParams(
            collective_id=1, has_side_effects=True, vmem_limit_bytes=59 * 2**20
        ),
        name="fetch_pool_and_tower",
    )(emb_table, req, bag_rows.reshape(1024, 128), placement_slot.reshape(1024, 4), w_hidden, w_out)


def tower(x, w_hidden, w_out):
    hidden = jnp.maximum(jnp.dot(x, w_hidden, preferred_element_type=jnp.float32), 0.0).astype(jnp.bfloat16)
    raw = jnp.dot(hidden, w_out, preferred_element_type=jnp.float32)
    scale = lax.rsqrt(jnp.mean(raw * raw, axis=-1, keepdims=True) + 1e-06)
    return (raw * scale).astype(jnp.bfloat16)


def pool_kernel(row_a, row_b, fetched, w_hidden, w_out, out, table, rows, x, chunk, sem):
    step = pl.program_id(0)

    @pl.when(step == 0)
    def _():
        table[pl.ds(ZERO_ROW, 8), :] = jnp.zeros((8, EMB), jnp.float32)
        pieces = CAP * DEVICES // 16

        def copy(n):
            return pltpu.make_async_copy(
                fetched.at[lax.div(n, 8), pl.ds(lax.rem(n, 8) * 16, 16)], chunk.at[lax.rem(n, 2)], sem.at[lax.rem(n, 2)]
            )

        copy(0).start()

        def load(n, _):
            @pl.when(n + 1 < pieces)
            def _():
                copy(n + 1).start()

            copy(n).wait()
            for k in range(16):
                at = pl.multiple_of((n * 16 + k) * ROWS, ROWS)
                table[pl.ds(at, ROWS), :] = chunk[lax.rem(n, 2), k].astype(jnp.float32)
            return 0

        lax.fori_loop(0, pieces, load, 0)

    def group(g, _):
        def some(t, _):
            for f in range(FEATS):
                a = row_a[t * FEATS + f, step * 16 + g]
                b = row_b[t * FEATS + f, step * 16 + g]
                rows[pl.ds(f * 16 + t, 1), :] = table[pl.ds(a, 1), :] + table[pl.ds(b, 1), :]
            return 0

        lax.fori_loop(0, 16, some, 0, unroll=2)
        at = pl.multiple_of(g * 16, 16)
        for f in range(FEATS):
            x[pl.ds(at, 16), f * EMB : (f + 1) * EMB] = rows[f * 16 : (f + 1) * 16, :].astype(jnp.bfloat16)
        return 0

    lax.fori_loop(0, 16, group, 0)
    out[...] = tower(x[...], w_hidden[...], w_out[...])


def pool(row_a, row_b, fetched, w_hidden, w_out):
    smem = pl.BlockSpec(memory_space=pltpu.SMEM)
    return pl.pallas_call(
        pool_kernel,
        grid=(N_DP,),
        in_specs=[
            smem,
            smem,
            pl.BlockSpec(memory_space=pl.ANY),
            pl.BlockSpec((2048, UNITS), lambda n: (0, 0), pipeline_mode=pl.Buffered(1)),
            pl.BlockSpec((UNITS, VEC), lambda n: (0, 0), pipeline_mode=pl.Buffered(1)),
        ],
        out_specs=pl.BlockSpec((SHARD, VEC), lambda n: (n, 0)),
        out_shape=jax.ShapeDtypeStruct((SLOTS, VEC), jnp.bfloat16),
        scratch_shapes=[
            pltpu.VMEM((TABLE_ROWS + 8, EMB), jnp.float32),
            pltpu.VMEM((GROUP, EMB), jnp.float32),
            pltpu.VMEM((SHARD, FEATS * EMB), jnp.bfloat16),
            pltpu.VMEM((2, 16, ROWS, EMB), jnp.bfloat16),
            pltpu.SemaphoreType.DMA((2,)),
        ],
        compiler_params=pltpu.CompilerParams(vmem_limit_bytes=58 * 2**20),
        name="pool_and_tower",
    )(row_a, row_b, fetched, w_hidden, w_out)


def local(emb_table, requests, bag_rows, placement_slot, w_hidden, w_out):
    vectors, fetched, row_a, row_b, late = fused(
        emb_table, requests, bag_rows, placement_slot, w_hidden, w_out
    )

    def general(vectors):
        again = pool(row_a, row_b, fetched, w_hidden, w_out).reshape(N_DP, SHARD, VEC)
        return lax.all_to_all(again, "dp", split_axis=0, concat_axis=0, tiled=True)

    vectors = lax.cond(jnp.max(late) > 0, general, lambda vectors: vectors, vectors)
    return vectors.reshape(SLOTS, VEC)


def solution(mesh):
    placed = (
        P(("dp", "table"), None, None),
        P(("dp", "table"), None),
        P(("dp", "table")),
        P(("dp", "table")),
        P(),
        P(),
    )
    return jax.shard_map(
        local, mesh=mesh, in_specs=placed, out_specs=P(("dp", "table"), None), check_vma=False
    )
```

```python
import itertools

import jax
import jax.numpy as jnp
import numpy as np
from jax import lax
from jax.experimental import pallas as pl
from jax.experimental.pallas import tpu as pltpu
from jax.sharding import PartitionSpec as P

MESH = pl.DeviceIdType.MESH
FEATS = 16
N_DP, N_TABLE = 8, 16
DEVICES = N_DP * N_TABLE
CAP = 3
ROWS = 128
EMB = 128
ITEMS = 4096
SLOTS = 2048
GROUP = 256
GROUPS = SLOTS * FEATS // GROUP
SHARD = SLOTS // N_DP
UNITS = 1024
VEC = 256
TABLE_ROWS = CAP * DEVICES * ROWS
ZERO_ROW = TABLE_ROWS

PHASES = 13
SCHEDULE = (16, 32, 48, 80, 112, 112, 128, 144, 144, 160, 176, 192, GROUP)

DISPLACEMENTS = [d for d in itertools.product(range(4), range(4), range(4), range(2)) if any(d)]


def hops(d):
    load = np.zeros(6)
    for axis in range(3):
        if d[axis] in (1, 2):
            load[2 * axis] += 1
        if d[axis] in (2, 3):
            load[2 * axis + 1] += 1
    return load


def balanced(left):
    left, out, total = list(left), [], np.zeros(6)
    mean = sum(hops(d).sum() for d in left) / len(left)
    rng = np.random.default_rng(0)

    def score(d):
        after = total + hops(d)
        value = 10 * (after.max() - after.min()) + ((after - after.mean()) ** 2).sum()
        return value + 0.3 * abs(after.sum() / (len(out) + 1) - mean) + 0.01 * rng.random()

    while left:
        best = min([(score(d), d) for d in left])[1]
        left.remove(best)
        out.append(best)
        total = total + hops(best)
    return out


def part_of(d):
    return ((d[1] - d[0]) % 4) * 2 + d[3]


def place_of(d):
    return part_of(d) * 16 + d[0] * 4 + (d[2] - d[0]) % 4


ORDER = balanced(DISPLACEMENTS)
ORDER_BY_PART = sum([balanced([d for d in DISPLACEMENTS if part_of(d) == k]) for k in range(8)], [])


def my_place():
    i, j = lax.axis_index("dp"), lax.axis_index("table")
    return lax.div(j, 4), lax.rem(j, 4), lax.div(i, 2), lax.rem(i, 2)


def moved(d, sign):
    x, y, z, core = my_place()
    x = lax.rem(x + (sign * d[0]) % 4, 4)
    y = lax.rem(y + (sign * d[1]) % 4, 4)
    z = lax.rem(z + (sign * d[2]) % 4, 4)
    core = lax.rem(core + d[3], 2)
    return z * 2 + core, x * 4 + y


def table_row(idx, present):
    x, y, z, core = my_place()
    block = idx >> 7
    owner = (block * 43691) >> 17
    slot = block - owner * 3
    dx = (x - ((owner >> 2) & 3)) & 3
    dy = (y - (owner & 3)) & 3
    dz = (z - (owner >> 5)) & 3
    dcore = (core - ((owner >> 4) & 1)) & 1
    part = ((dy - dx) & 3) * 2 + dcore
    place = part * 16 + dx * 4 + ((dz - dx) & 3)
    row = ((slot * DEVICES + place) << 7) | (idx & 127)
    phase = jnp.where(slot == 2, 5 + part, jnp.where(slot == 1, 1 + (part >> 1), 0))
    return jnp.where(present, row, ZERO_ROW), jnp.where(present, phase, 0)


def pick_bags(bags_ref, placed_ref, bag_t, picked):
    bag_t[...] = jnp.transpose(bags_ref[...])
    ones = jnp.ones((8, 1024), jnp.float32)

    def chunk(n, _):
        lane = lax.broadcasted_iota(jnp.int32, (1024, 256), 1) + n * 256
        wanted = (lane & 127) * 16 + (lane >> 7)
        total = jnp.zeros((72, 256), jnp.float32)
        for q in range(4):
            hit = placed_ref[:, q : q + 1] == wanted
            hit = jnp.where(hit, 1.0, 0.0).astype(jnp.bfloat16)
            bag = bag_t[q * 32 : (q + 1) * 32, :]
            left = jnp.concatenate([(bag >> 8).astype(jnp.float32), (bag & 255).astype(jnp.float32), ones])
            total += jnp.dot(left.astype(jnp.bfloat16), hit, preferred_element_type=jnp.float32)
        picked[2 * n] = total[:, :128]
        picked[2 * n + 1] = total[:, 128:]
        return 0

    lax.fori_loop(0, SLOTS // 256, chunk, 0)


def bag_matrix(picked, entry):
    rows, live = [], []
    for t in range(16):
        high = picked[t, pl.ds(entry, 16, stride=2), :]
        low = picked[t, pl.ds(32 + entry, 16, stride=2), :]
        rows.append(high.astype(jnp.int32) * 256 + low.astype(jnp.int32))
        there = picked[t, 64:72, :] > 0.5
        live.append(jnp.concatenate([jnp.where(there, 1, 0)] * 2))
    return jnp.concatenate(rows), jnp.concatenate(live) > 0


def sort_rows(key, load):
    row = lax.broadcasted_iota(jnp.int32, (GROUP, GROUPS), 0)
    size = 2
    while size <= GROUP:
        step = size // 2
        while step:
            lower = (row & step) == 0
            other_key = jnp.where(lower, pltpu.roll(key, GROUP - step, 0), pltpu.roll(key, step, 0))
            other_load = jnp.where(lower, pltpu.roll(load, GROUP - step, 0), pltpu.roll(load, step, 0))
            keeps_least = lower == ((row & size) == 0)
            swap = keeps_least == (other_key < key)
            key = jnp.where(swap, other_key, key)
            load = jnp.where(swap, other_load, load)
            step //= 2
        size *= 2
    return key, load


def fused_kernel(
    emb, req, bags, placed, w_hidden, w_out,
    out, fetched, row_a, row_b, late,
    blocks, staged, table, req_in, req_s, bag_t, picked, sorted_a, sorted_b, order_t, rows_a, rows_b,
    chunk, rows, x, vectors, flags,
    emb_sem, req_send, req_recv, own_sem, send_sem, recv_sem, chunk_sem, flag_send, flag_recv, vec_send, vec_recv,
):
    me_dp, me_table = lax.axis_index("dp"), lax.axis_index("table")
    load = pltpu.make_async_copy(emb, blocks, emb_sem)
    load.start()
    barrier = pltpu.get_barrier_semaphore()
    for d in ORDER:
        pl.semaphore_signal(barrier, inc=1, device_id=moved(d, 1), device_id_type=MESH)
    pl.semaphore_wait(barrier, DEVICES - 1)

    own = pltpu.make_async_copy(req.at[me_dp * N_TABLE + me_table], req_in.at[0], own_sem)
    own.start()
    for d in ORDER:
        to = moved(d, -1)
        pltpu.make_async_remote_copy(
            src_ref=req.at[to[0] * N_TABLE + to[1]], dst_ref=req_in.at[place_of(d)],
            send_sem=req_send, recv_sem=req_recv, device_id=to, device_id_type=MESH,
        ).start()
    own.wait()
    others = req_in.at[pl.ds(1, DEVICES - 1)]
    pltpu.make_async_copy(others, others, req_recv).wait()
    pltpu.make_async_copy(others, others, req_send).wait()
    numbers = pltpu.make_async_copy(req_in, req_s, own_sem)
    numbers.start()
    load.wait()
    numbers.wait()

    def send(slot):
        room = slot % 2

        def serve(n, _):
            number = req_s[n, 0, slot]
            block = blocks[jnp.maximum(number, 0)]
            staged[room, n] = jnp.where(number >= 0, block, jnp.zeros_like(block))
            return 0

        lax.fori_loop(0, DEVICES, serve, 0)
        for d in ORDER_BY_PART if slot else ORDER:
            n = place_of(d)
            phase = (0, 1 + part_of(d) // 2, 5 + part_of(d))[slot]
            pltpu.make_async_remote_copy(
                src_ref=staged.at[room, n], dst_ref=fetched.at[slot, n], send_sem=send_sem.at[slot],
                recv_sem=recv_sem.at[phase], device_id=moved(d, 1), device_id_type=MESH,
            ).start()
        mine = pltpu.make_async_copy(staged.at[room, 0], fetched.at[slot, 0], own_sem)
        mine.start()
        mine.wait()

    def sent(slot):
        room = staged.at[slot % 2, pl.ds(1, DEVICES - 1)]
        pltpu.make_async_copy(room, room, send_sem.at[slot]).wait()

    send(0)

    table[pl.ds(ZERO_ROW, 8), :] = jnp.zeros((8, EMB), jnp.float32)
    pick_bags(bags, placed, bag_t, picked)
    idx_a, present = bag_matrix(picked, 0)
    idx_b, _ = bag_matrix(picked, 1)
    idx_a, phase_a = table_row(idx_a, present)
    idx_b, phase_b = table_row(idx_b, present)
    row_a[...] = idx_a
    row_b[...] = idx_b
    row = lax.broadcasted_iota(jnp.int32, (GROUP, GROUPS), 0)
    key = jnp.maximum(phase_a, phase_b) * GROUP + (row & 15) * 16 + (row >> 4)
    key, pair = sort_rows(key, idx_a | (idx_b << 16))
    sorted_a[...] = jnp.minimum(pair & 65535, ZERO_ROW)
    sorted_b[...] = jnp.minimum((pair >> 16) & 65535, ZERO_ROW)
    order_t[...] = jnp.transpose(key & (GROUP - 1))
    to_a = pltpu.make_async_copy(sorted_a, rows_a, chunk_sem.at[0])
    to_b = pltpu.make_async_copy(sorted_b, rows_b, chunk_sem.at[1])
    to_a.start()
    to_b.start()
    limit = jnp.zeros_like(row)
    for end in SCHEDULE[:-1]:
        limit += jnp.where(row >= end, 1, 0)
    missed = jnp.max(jnp.where((key >> 8) > limit, 1.0, 0.0), axis=0, keepdims=True)
    missed = jnp.max(missed, axis=1, keepdims=True).astype(jnp.int32)
    flags[0] = jnp.broadcast_to(missed, (8, GROUPS))
    to_a.wait()
    to_b.wait()

    def share(first, count, device):
        copies = []
        for s in range(1, count):
            copies.append(
                pltpu.make_async_remote_copy(
                    src_ref=flags.at[first], dst_ref=flags.at[first + s], send_sem=flag_send.at[first + s],
                    recv_sem=flag_recv.at[first + s], device_id=device(s), device_id_type=MESH,
                )
            )
            copies[-1].start()
        return copies

    def gather_flags(copies, first, count):
        for c in copies:
            c.wait()
        total = flags[first]
        for s in range(1, count):
            total = jnp.maximum(total, flags[first + s])
        return total

    def arrive(slot, first, count):
        pieces = count // 16

        def copy(n):
            return pltpu.make_async_copy(
                fetched.at[slot, pl.ds(first + n * 16, 16)], chunk.at[lax.rem(n, 2)], chunk_sem.at[lax.rem(n, 2)]
            )

        def convert(n):
            copy(n).wait()
            for k in range(16):
                at = pl.multiple_of((slot * DEVICES + first + n * 16 + k) * ROWS, ROWS)
                table[pl.ds(at, ROWS), :] = chunk[lax.rem(n, 2), k].astype(jnp.float32)

        copy(0).start()

        def piece(n, _):
            copy(n + 1).start()
            convert(n)
            return 0

        lax.fori_loop(0, pieces - 1, piece, 0)
        convert(pieces - 1)

    def add_rows(g, low, high, at):
        for n in range(low, high):
            a, b = rows_a[n, g], rows_b[n, g]
            rows[at, n - low : n - low + 1, :] = table[pl.ds(a, 1), :] + table[pl.ds(b, 1), :]

    def pool_some(low, high):
        half, first = low // 128, low % 128
        step = 2 if high - low < 32 else 1

        def eight(n, _):
            def one(m, _):
                for k in range(step):
                    add_rows(n * 8 + m * step + k, low, high, m * step + k)
                return 0

            lax.fori_loop(0, 8 // step, one, 0)
            for m in range(8):
                blocks[(n * 8 + m) * 2 + half, first : first + high - low, :] = rows[m, : high - low, :].astype(
                    jnp.bfloat16
                )
            return 0

        lax.fori_loop(0, GROUPS // 8, eight, 0)

    def phase_done(phase):
        if phase == 0:
            slot, first, count = 0, 0, DEVICES
        elif phase < 5:
            slot, first, count = 1, (phase - 1) * 32, 32
        else:
            slot, first, count = 2, (phase - 5) * 16, 16
        skip = 1 if first == 0 else 0
        arrived = fetched.at[slot, pl.ds(first + skip, count - skip)]
        pltpu.make_async_copy(arrived, arrived, recv_sem.at[phase]).wait()
        arrive(slot, first, count)

    flag_copies = share(0, N_DP, lambda s: (lax.rem(me_dp + s, N_DP), me_table))
    sent(0)
    send(1)
    done = 0
    for phase in range(PHASES - 1):
        phase_done(phase)
        if phase == 0:
            send(2)
        if SCHEDULE[phase] > done:
            pool_some(done, SCHEDULE[phase])
            done = SCHEDULE[phase]
    phase_done(PHASES - 1)
    flags[8] = gather_flags(flag_copies, 0, N_DP)
    flag_copies = share(8, N_TABLE, lambda s: (me_dp, lax.rem(me_table + s, N_TABLE)))

    lane = lax.broadcasted_iota(jnp.int32, (GROUP, GROUP), 0)

    def shard(s, _):
        k = lax.rem(me_dp + 1 + s, N_DP)

        def last_rows(n, _):
            def one(m, _):
                add_rows(k * 16 + n * 8 + m, done, GROUP, m)
                return 0

            lax.fori_loop(0, 8, one, 0)
            for m in range(8):
                blocks[(k * 16 + n * 8 + m) * 2 + 1, done - 128 :, :] = rows[m, : GROUP - done, :].astype(jnp.bfloat16)
            return 0

        lax.fori_loop(0, 2, last_rows, 0)

        def in_place(n, _):
            for m in range(8):
                g = k * 16 + n * 8 + m
                pick = jnp.where(order_t[pl.ds(g, 1), :] == lane, 1.0, 0.0).astype(jnp.bfloat16)
                pooled = jnp.concatenate([blocks[2 * g], blocks[2 * g + 1]])
                pooled = jnp.dot(pick, pooled, preferred_element_type=jnp.float32).astype(jnp.bfloat16)
                at = pl.multiple_of((n * 8 + m) * 16, 16)
                for f in range(FEATS):
                    x[pl.ds(at, 16), f * EMB : (f + 1) * EMB] = pooled[f * 16 : (f + 1) * 16, :]
            return 0

        lax.fori_loop(0, 2, in_place, 0)
        vectors[k] = tower(x[...], w_hidden[...], w_out[...])

        @pl.when(s < N_DP - 1)
        def _():
            pltpu.make_async_remote_copy(
                src_ref=vectors.at[k], dst_ref=out.at[me_dp], send_sem=vec_send.at[s],
                recv_sem=vec_recv.at[me_dp], device_id=(k, me_table), device_id_type=MESH,
            ).start()

        return 0

    lax.fori_loop(0, N_DP, shard, 0)
    late[...] = gather_flags(flag_copies, 8, N_TABLE)
    last = pltpu.make_async_copy(vectors.at[me_dp], out.at[me_dp], own_sem)
    last.start()
    sent(1)
    sent(2)
    for s in range(1, N_DP):
        k = lax.rem(me_dp + s, N_DP)
        pltpu.make_async_copy(vectors.at[k], vectors.at[k], vec_send.at[s - 1]).wait()
        pltpu.make_async_copy(out.at[k], out.at[k], vec_recv.at[k]).wait()
    last.wait()


def fused(emb_table, requests, bag_rows, placement_slot, w_hidden, w_out):
    req = jnp.pad(requests, ((0, 0), (0, 125))).reshape(DEVICES, 1, 128)
    hbm = pl.BlockSpec(memory_space=pl.ANY)
    vmem = pl.BlockSpec(memory_space=pltpu.VMEM)
    dma = pltpu.SemaphoreType.DMA
    return pl.pallas_call(
        fused_kernel,
        in_specs=[hbm, vmem, vmem, vmem, vmem, vmem],
        out_specs=(hbm, hbm, vmem, vmem, vmem),
        out_shape=(
            jax.ShapeDtypeStruct((N_DP, SHARD, VEC), jnp.bfloat16),
            jax.ShapeDtypeStruct((CAP, DEVICES, ROWS, EMB), jnp.bfloat16),
            jax.ShapeDtypeStruct((GROUP, GROUPS), jnp.int32),
            jax.ShapeDtypeStruct((GROUP, GROUPS), jnp.int32),
            jax.ShapeDtypeStruct((8, GROUPS), jnp.int32),
        ),
        scratch_shapes=[
            pltpu.VMEM((256, ROWS, EMB), jnp.bfloat16),
            pltpu.VMEM((2, DEVICES, ROWS, EMB), jnp.bfloat16),
            pltpu.VMEM((TABLE_ROWS + 8, EMB), jnp.float32),
            pltpu.VMEM((DEVICES, 1, 128), jnp.int32),
            pltpu.SMEM((DEVICES, 1, 128), jnp.int32),
            pltpu.VMEM((128, 1024), jnp.int32),
            pltpu.VMEM((16, 72, 128), jnp.float32),
            pltpu.VMEM((GROUP, GROUPS), jnp.int32),
            pltpu.VMEM((GROUP, GROUPS), jnp.int32),
            pltpu.VMEM((GROUPS, GROUP), jnp.int32),
            pltpu.SMEM((GROUP, GROUPS), jnp.int32),
            pltpu.SMEM((GROUP, GROUPS), jnp.int32),
            pltpu.VMEM((2, 16, ROWS, EMB), jnp.bfloat16),
            pltpu.VMEM((8, 96, EMB), jnp.float32),
            pltpu.VMEM((SHARD, FEATS * EMB), jnp.bfloat16),
            pltpu.VMEM((N_DP, SHARD, VEC), jnp.bfloat16),
            pltpu.VMEM((24, 8, GROUPS), jnp.int32),
            dma, dma, dma, dma, dma((CAP,)),
            dma((PHASES,)), dma((2,)), dma((24,)), dma((24,)), dma((N_DP,)), dma((N_DP,)),
        ],
        compiler_params=pltpu.CompilerParams(
            collective_id=1, has_side_effects=True, vmem_limit_bytes=59 * 2**20
        ),
        name="fetch_pool_and_tower",
    )(emb_table, req, bag_rows.reshape(1024, 128), placement_slot.reshape(1024, 4), w_hidden, w_out)


def tower(x, w_hidden, w_out):
    hidden = jnp.maximum(jnp.dot(x, w_hidden, preferred_element_type=jnp.float32), 0.0).astype(jnp.bfloat16)
    raw = jnp.dot(hidden, w_out, preferred_element_type=jnp.float32)
    scale = lax.rsqrt(jnp.mean(raw * raw, axis=-1, keepdims=True) + 1e-06)
    return (raw * scale).astype(jnp.bfloat16)


def pool_kernel(row_a, row_b, fetched, w_hidden, w_out, out, table, rows, x, chunk, sem):
    step = pl.program_id(0)

    @pl.when(step == 0)
    def _():
        table[pl.ds(ZERO_ROW, 8), :] = jnp.zeros((8, EMB), jnp.float32)
        pieces = CAP * DEVICES // 16

        def copy(n):
            return pltpu.make_async_copy(
                fetched.at[lax.div(n, 8), pl.ds(lax.rem(n, 8) * 16, 16)], chunk.at[lax.rem(n, 2)], sem.at[lax.rem(n, 2)]
            )

        copy(0).start()

        def load(n, _):
            @pl.when(n + 1 < pieces)
            def _():
                copy(n + 1).start()

            copy(n).wait()
            for k in range(16):
                at = pl.multiple_of((n * 16 + k) * ROWS, ROWS)
                table[pl.ds(at, ROWS), :] = chunk[lax.rem(n, 2), k].astype(jnp.float32)
            return 0

        lax.fori_loop(0, pieces, load, 0)

    def group(g, _):
        def some(t, _):
            for f in range(FEATS):
                a = row_a[t * FEATS + f, step * 16 + g]
                b = row_b[t * FEATS + f, step * 16 + g]
                rows[pl.ds(f * 16 + t, 1), :] = table[pl.ds(a, 1), :] + table[pl.ds(b, 1), :]
            return 0

        lax.fori_loop(0, 16, some, 0, unroll=2)
        at = pl.multiple_of(g * 16, 16)
        for f in range(FEATS):
            x[pl.ds(at, 16), f * EMB : (f + 1) * EMB] = rows[f * 16 : (f + 1) * 16, :].astype(jnp.bfloat16)
        return 0

    lax.fori_loop(0, 16, group, 0)
    out[...] = tower(x[...], w_hidden[...], w_out[...])


def pool(row_a, row_b, fetched, w_hidden, w_out):
    smem = pl.BlockSpec(memory_space=pltpu.SMEM)
    return pl.pallas_call(
        pool_kernel,
        grid=(N_DP,),
        in_specs=[
            smem,
            smem,
            pl.BlockSpec(memory_space=pl.ANY),
            pl.BlockSpec((2048, UNITS), lambda n: (0, 0), pipeline_mode=pl.Buffered(1)),
            pl.BlockSpec((UNITS, VEC), lambda n: (0, 0), pipeline_mode=pl.Buffered(1)),
        ],
        out_specs=pl.BlockSpec((SHARD, VEC), lambda n: (n, 0)),
        out_shape=jax.ShapeDtypeStruct((SLOTS, VEC), jnp.bfloat16),
        scratch_shapes=[
            pltpu.VMEM((TABLE_ROWS + 8, EMB), jnp.float32),
            pltpu.VMEM((GROUP, EMB), jnp.float32),
            pltpu.VMEM((SHARD, FEATS * EMB), jnp.bfloat16),
            pltpu.VMEM((2, 16, ROWS, EMB), jnp.bfloat16),
            pltpu.SemaphoreType.DMA((2,)),
        ],
        compiler_params=pltpu.CompilerParams(vmem_limit_bytes=58 * 2**20),
        name="pool_and_tower",
    )(row_a, row_b, fetched, w_hidden, w_out)


def local(emb_table, requests, bag_rows, placement_slot, w_hidden, w_out):
    vectors, fetched, row_a, row_b, late = fused(
        emb_table, requests, bag_rows, placement_slot, w_hidden, w_out
    )

    def general(vectors):
        again = pool(row_a, row_b, fetched, w_hidden, w_out).reshape(N_DP, SHARD, VEC)
        return lax.all_to_all(again, "dp", split_axis=0, concat_axis=0, tiled=True)

    vectors = lax.cond(late[0, 0] > 0, general, lambda vectors: vectors, vectors)
    return vectors.reshape(SLOTS, VEC)


def solution(mesh):
    placed = (
        P(("dp", "table"), None, None),
        P(("dp", "table"), None),
        P(("dp", "table")),
        P(("dp", "table")),
        P(),
        P(),
    )
    return jax.shard_map(
        local, mesh=mesh, in_specs=placed, out_specs=P(("dp", "table"), None), check_vma=False
    )
```
